32 devices in a mesh: eg: 8 (over z, x), blk: 4 (over y, core).
Axes of the slice: x: 2, y: 2, z: 4, core: 2. Of those that a mesh axis runs over, the one named last changes fastest.
Arguments:
- tokens: bfloat16 [256, 7168], P(('eg', 'blk')), may hold values from -6 to 6
- grad_out: bfloat16 [256, 7168], P(('eg', 'blk')), may hold values from -4 to 4
- expert_ids: int32 [256, 2], P(('eg', 'blk')), may hold values from 0 to 7, all different within a row; in each aligned block of 8 rows (0 to 7, 8 to 15, ...) at most 4 rows name the same one
- gate_weights: bfloat16 [256, 2], P(('eg', 'blk')), may hold values from 0.049804688 to 1
- gate_codes: bfloat16 [8, 7168, 2048], P('eg', None, 'blk'), may hold values from -0.0625 to 0.0625
- up_codes: bfloat16 [8, 7168, 2048], P('eg', None, 'blk'), may hold values from -0.0625 to 0.0625
- down_codes: bfloat16 [8, 7168, 2048], P('eg', None, 'blk'), may hold values from -0.125 to 0.125
- block_scales: bfloat16 [8, 3, 16, 56], P('eg', None, 'blk'), may hold values from 0.29882812 to 3
Outputs:
- grad_tokens: bfloat16 [256, 7168], P(('eg', 'blk'))
- grad_gates: bfloat16 [256, 2], P(('eg', 'blk'))
- gate_grad: bfloat16 [8, 7168, 2048], P('eg', None, 'blk')
- up_grad: bfloat16 [8, 7168, 2048], P('eg', None, 'blk')
- down_grad: bfloat16 [8, 7168, 2048], P('eg', None, 'blk')
The draws below stay inside these ranges and needn't reach their ends.
Inputs may be any that keep to these rules, and one draw needn't show every extreme that they name: `expert_ids`: each token names 2 different experts. Among the 8 tokens of one device (aligned blocks of rows) at most 4 name the same expert, and in every draw some device's tokens reach 4 for some expert.
All inputs are finite; a program needn't handle non-finite values.
Results may differ from the reference program's by a relative error of at most 0.028.
Values may be sent and summed in bfloat16 or wider, within the bound.
A program may use at most 128 MiB of HBM per device.

```python
import math
import jax
import jax.numpy as jnp
import numpy as np
from jax import lax

D = 7168
HID = 2048
QBLOCK = 128
TOPK = 2
TOK_DEV = 8
EXPERTS = 8
CAP = 4
TOKENS = 256
N_EG = 8
N_BLK = 4


def shard_levels(stream_key, extent, pieces, least, top_value):
    factor_of = 1.0
    for dim, shards_of in pieces:
        steps = jax.random.uniform(jax.random.fold_in(jax.random.fold_in(stream_key, 6), dim), (shards_of,), jnp.float32, least / len(pieces), top_value / len(pieces))
        factor_of = factor_of * jnp.repeat(jnp.exp(steps), extent[dim] // shards_of).reshape((-1,) + (1,) * (len(extent) - 1 - dim))
    return factor_of


def assign_block(own_key, own, number, rows, amount, top, bound, slope):
    order = jax.random.permutation(own_key, amount)
    crowded, common = portions_of(amount, rows * top, bound, slope, True), portions_of(amount, rows * top, bound, slope, False)
    places = jnp.arange(amount)

    def named(sizes, rotation):
        used = int((sizes > 0).sum())
        fixed = max(1, used // 4)
        shifted = fixed + (places - fixed + rotation * (used - fixed)) % max(1, amount - fixed)
        return jnp.zeros((amount,), jnp.int32).at[order[jnp.where(places < fixed, places, shifted)]].set(jnp.asarray(sizes, jnp.int32))

    sizes = jnp.where(number % 4 == 0, named(crowded, number // 4), named(common, number - number // 4 - 1))
    mixed = jax.random.permutation(jax.random.fold_in(own, 3), amount)
    donor, sink = mixed[0:amount // 2 * 2:2], mixed[1:amount // 2 * 2:2]
    margin = jnp.minimum(sizes[donor] - 1, bound - sizes[sink]) // 2
    margin = jnp.where((donor == order[0]) | (sink == order[0]) | (sizes[sink] == 0), 0, jnp.maximum(margin, 0))
    shifted = jax.random.randint(jax.random.fold_in(own, 4), (amount // 2,), 0, 1 << 20) % (margin + 1)
    sizes = sizes.at[donor].add(-shifted).at[sink].add(shifted)
    labels = jnp.searchsorted(jnp.cumsum(sizes), jnp.arange(rows * top), side="right").astype(jnp.int32)
    listing = labels.reshape(top, rows).T
    listing = listing[jax.random.permutation(jax.random.fold_in(own, 1), rows)]
    rotation = jax.random.randint(jax.random.fold_in(own, 2), (rows, 1), 0, top)
    return jnp.take_along_axis(listing, (jnp.arange(top)[None, :] + rotation) % top, axis=1)


def portions_of(amount, total, limit, skew, full):
    loads = [(1 << 20) // math.isqrt(standing ** skew) + 1 for standing in range(1, amount + 1)]
    largest = limit if full else min(limit, max(-(-total // amount), total * loads[0] // sum(loads)))
    least = 1 if total - largest >= amount - 1 else 0
    given, rest = [largest] + [least] * (amount - 1), total - largest - least * (amount - 1)
    while rest > 0:
        free = [i for i in range(1, amount) if given[i] < largest] or [i for i in range(1, amount) if given[i] < limit]
        mass, budget = sum([loads[i] for i in free]), rest
        for i in free:
            addition = min(limit - given[i], max(1, budget * loads[i] // mass), rest)
            given[i] = given[i] + addition
            rest = rest - addition
    return np.array(given)


def normal_values(stream_key, dims, scale, reach, shards=(), held_as=jnp.bfloat16):
    array = scale * jax.random.normal(stream_key, dims, jnp.float32)
    if shards:
        array = array * shard_levels(stream_key, dims, shards, -0.22, 0.18)
    return jnp.clip(array, -reach, reach).astype(held_as)


def setup_inputs(seed: int = 0) -> dict:
    seeds = jax.random.split(jax.random.key(seed), 9)
    tokens = normal_values(seeds[0], (TOKENS, D), 1.0, 6.0, ((0, 32),))
    grad_out = normal_values(seeds[1], (TOKENS, D), 0.5, 4.0, ((0, 32),))
    expert_ids_keys = jax.random.split(jax.random.fold_in(seeds[2], 1), TOKENS // TOK_DEV)
    expert_ids_turns = jax.random.permutation(jax.random.fold_in(seeds[2], 3), TOKENS // TOK_DEV)
    expert_ids = jax.vmap(lambda own, number: assign_block(jax.random.fold_in(seeds[2], 2), own, number, TOK_DEV, EXPERTS, TOPK, CAP, 2))(expert_ids_keys, expert_ids_turns).reshape((TOKENS, TOPK))
    gate_weights = jnp.clip(jnp.exp(math.log(1.0) - 2.9996462 * jax.random.uniform(seeds[3], (TOKENS, TOPK), jnp.float32) ** shard_levels(seeds[3], (TOKENS, TOPK), ((0, 32),), -0.2, 0.2)), 0.049804688, 1.0).astype(jnp.bfloat16)
    gate_codes = normal_values(seeds[4], (EXPERTS, D, HID), D ** -0.5, 0.0625, ((0, 8), (2, 4)))
    up_codes = normal_values(seeds[5], (EXPERTS, D, HID), D ** -0.5, 0.0625, ((0, 8), (2, 4)))
    down_codes = normal_values(seeds[6], (EXPERTS, D, HID), HID ** -0.5, 0.125, ((0, 8), (2, 4)))
    block_scales = jnp.clip(jnp.exp(math.log(3.0) - 2.306499 * jax.random.uniform(seeds[7], (EXPERTS, 3, HID // QBLOCK, D // QBLOCK), jnp.float32) ** shard_levels(seeds[7], (EXPERTS, 3, HID // QBLOCK, D // QBLOCK), ((0, 8), (2, 4)), -0.2, 0.2)), 0.29882812, 3.0).astype(jnp.bfloat16)
    return dict(tokens=tokens, grad_out=grad_out, expert_ids=expert_ids, gate_weights=gate_weights, gate_codes=gate_codes, up_codes=up_codes, down_codes=down_codes, block_scales=block_scales)


def dequantize(codes, scales):
    rows_in, cols_in = codes.shape
    blocks = codes.astype(jnp.float32).reshape(rows_in // QBLOCK, QBLOCK, cols_in // QBLOCK, QBLOCK)
    scaled = blocks * jnp.transpose(scales.astype(jnp.float32))[:, None, :, None]
    return scaled.reshape(rows_in, cols_in).astype(jnp.bfloat16)


def backward_math(gate_pre, up_pre, down_back, gates):
    sigma = jax.nn.sigmoid(gate_pre)
    hidden = gate_pre * sigma * up_pre
    grad_hidden = gates[:, None] * down_back
    grad_up = (grad_hidden * gate_pre * sigma).astype(jnp.bfloat16)
    grad_gate = (grad_hidden * up_pre * sigma * (1.0 + gate_pre * (1.0 - sigma))).astype(jnp.bfloat16)
    gated_hidden = (gates[:, None] * hidden).astype(jnp.bfloat16)
    return hidden, grad_gate, grad_up, gated_hidden


def reference(tokens, grad_out, expert_ids, gate_weights, gate_codes, up_codes, down_codes, block_scales):
    span = N_EG * N_BLK * CAP
    width = tokens.shape[1]
    flat = expert_ids.reshape(-1).astype(jnp.int32)
    order = jnp.argsort(flat, stable=True).astype(jnp.int32)
    counts = jnp.sum((flat[:, None] == jnp.arange(EXPERTS, dtype=jnp.int32)[None, :]).astype(jnp.int32), axis=0)
    offsets = (jnp.cumsum(counts) - counts).astype(jnp.int32)
    padded = jnp.concatenate([order, jnp.zeros((span,), jnp.int32)])
    hidden_local = HID // N_BLK
    contract_cols = (((1,), (1,)), ((), ()))
    contract_rows = (((0,), (0,)), ((), ()))

    def one_expert(expert):
        picks = lax.dynamic_slice_in_dim(padded, offsets[expert].astype(jnp.int32), span)
        valid = jnp.arange(span, dtype=jnp.int32) < counts[expert]
        rows_tok = (picks // TOPK).astype(jnp.int32)
        rows_pick = (picks % TOPK).astype(jnp.int32)
        feats = jnp.where(valid[:, None], tokens[rows_tok], jnp.zeros_like(tokens[rows_tok]))
        cotan = jnp.where(valid[:, None], grad_out[rows_tok], jnp.zeros_like(grad_out[rows_tok]))
        gates = jnp.where(valid, gate_weights[rows_tok, rows_pick].astype(jnp.float32), jnp.float32(0.0))
        wgate = dequantize(gate_codes[expert], block_scales[expert, 0])
        wup = dequantize(up_codes[expert], block_scales[expert, 1])
        wdown = dequantize(down_codes[expert], block_scales[expert, 2])
        gate_pre = jnp.dot(feats, wgate, preferred_element_type=jnp.float32)
        up_pre = jnp.dot(feats, wup, preferred_element_type=jnp.float32)
        down_back = jnp.dot(cotan, wdown, preferred_element_type=jnp.float32)
        hidden, grad_gate, grad_up, gated_hidden = backward_math(gate_pre, up_pre, down_back, gates)
        contrib = jnp.zeros((span, width), jnp.float32)
        gate_sum = jnp.zeros((span,), jnp.float32)
        for number in range(N_BLK):
            lower = number * hidden_local
            upper = lower + hidden_local
            partial_value = lax.dot_general(grad_gate[:, lower:upper], wgate[:, lower:upper], contract_cols, preferred_element_type=jnp.float32)
            partial_value = partial_value + lax.dot_general(grad_up[:, lower:upper], wup[:, lower:upper], contract_cols, preferred_element_type=jnp.float32)
            contrib = contrib + lax.optimization_barrier(partial_value.astype(jnp.bfloat16)).astype(jnp.float32)
            scores = jnp.sum(hidden[:, lower:upper] * down_back[:, lower:upper], axis=1)
            gate_sum = gate_sum + lax.optimization_barrier(scores.astype(jnp.bfloat16)).astype(jnp.float32)
        gate_grad = lax.dot_general(feats, grad_gate, contract_rows, preferred_element_type=jnp.float32).astype(jnp.bfloat16)
        up_grad = lax.dot_general(feats, grad_up, contract_rows, preferred_element_type=jnp.float32).astype(jnp.bfloat16)
        down_grad = lax.dot_general(cotan, gated_hidden, contract_rows, preferred_element_type=jnp.float32).astype(jnp.bfloat16)
        return contrib.astype(jnp.bfloat16), gate_sum.astype(jnp.bfloat16), gate_grad, up_grad, down_grad, rows_tok, rows_pick, valid

    results = lax.map(one_expert, jnp.arange(EXPERTS, dtype=jnp.int32))
    contrib, gate_sum, gate_grad, up_grad, down_grad, rows_tok, rows_pick, valid = results
    contrib_f = jnp.where(valid[:, :, None], contrib.astype(jnp.float32), jnp.float32(0.0))
    grad_tokens = jnp.zeros((tokens.shape[0], width), jnp.float32)
    grad_tokens = grad_tokens.at[rows_tok.reshape(-1)].add(contrib_f.reshape(-1, width))
    gate_f = jnp.where(valid, gate_sum.astype(jnp.float32), jnp.float32(0.0))
    grad_gates = jnp.zeros((tokens.shape[0], TOPK), jnp.float32)
    grad_gates = grad_gates.at[rows_tok.reshape(-1), rows_pick.reshape(-1)].add(gate_f.reshape(-1))
    return (grad_tokens.astype(jnp.bfloat16), grad_gates.astype(jnp.bfloat16), gate_grad, up_grad, down_grad)
```

```python
import jax
import jax.numpy as jnp
from jax import lax
from jax.sharding import PartitionSpec as P

QBLOCK = 128
TOPK = 2


def dequantize(codes, scales):
    rows_in, cols_in = codes.shape
    blocks = codes.astype(jnp.float32).reshape(rows_in // QBLOCK, QBLOCK, cols_in // QBLOCK, QBLOCK)
    scaled = blocks * jnp.transpose(scales.astype(jnp.float32))[:, None, :, None]
    return scaled.reshape(rows_in, cols_in).astype(jnp.bfloat16)


def backward_math(gate_pre, up_pre, down_back, gates):
    sigma = jax.nn.sigmoid(gate_pre)
    hidden = gate_pre * sigma * up_pre
    grad_hidden = gates[:, None] * down_back
    grad_up = (grad_hidden * gate_pre * sigma).astype(jnp.bfloat16)
    grad_gate = (grad_hidden * up_pre * sigma * (1.0 + gate_pre * (1.0 - sigma))).astype(
        jnp.bfloat16
    )
    gated_hidden = (gates[:, None] * hidden).astype(jnp.bfloat16)
    return (hidden, grad_gate, grad_up, gated_hidden)


def routing_tables(expert_ids, experts, capacity):
    route_hot = (
        expert_ids[:, :, None] == jnp.arange(experts, dtype=jnp.int32)[None, None, :]
    ).astype(jnp.int32)
    chosen = jnp.sum(route_hot, axis=1)
    rows = jnp.arange(expert_ids.shape[0], dtype=jnp.int32)
    before = (rows[None, :] < rows[:, None]).astype(jnp.int32)
    earlier = jnp.sum(before[:, :, None] * chosen[None, :, :], axis=1)
    slot_hot = (earlier[:, :, None] == jnp.arange(capacity, dtype=jnp.int32)[None, None, :]).astype(
        jnp.int32
    )
    placed = chosen[:, :, None] * slot_hot
    picked = route_hot[:, :, :, None] * slot_hot[:, None, :, :]
    return (placed.astype(jnp.float32), picked.astype(jnp.float32))


def project_back(grad_gate, grad_up, wgate, wup):
    contract_cols = (((1,), (1,)), ((), ()))
    partial_value = lax.dot_general(
        grad_gate, wgate, contract_cols, preferred_element_type=jnp.float32
    )
    return partial_value + lax.dot_general(
        grad_up, wup, contract_cols, preferred_element_type=jnp.float32
    )


def row_sum(left, right):
    return lax.dot_general(
        left, right, (((0,), (0,)), ((), ())), preferred_element_type=jnp.float32
    )


def on_device(
    tokens, grad_out, expert_ids, gate_weights, gate_codes, up_codes, down_codes, block_scales
):
    experts = lax.axis_size("eg")
    width = tokens.shape[1]
    capacity = 2 * tokens.shape[0] * TOPK // experts
    placed, picked = routing_tables(expert_ids, experts, capacity)
    placed_low = placed.astype(jnp.bfloat16)
    send_tokens = jnp.einsum(
        "tec,td->ecd", placed_low, tokens, preferred_element_type=jnp.float32
    ).astype(jnp.bfloat16)
    send_cotan = jnp.einsum(
        "tec,td->ecd", placed_low, grad_out, preferred_element_type=jnp.float32
    ).astype(jnp.bfloat16)
    send_gates = jnp.einsum(
        "tkec,tk->ec", picked, gate_weights.astype(jnp.float32), precision=lax.Precision.HIGHEST
    ).astype(jnp.bfloat16)
    recv_tokens, recv_cotan, recv_gates = (
        lax.all_to_all(send_tokens, "eg", split_axis=0, concat_axis=0, tiled=True),
        lax.all_to_all(send_cotan, "eg", split_axis=0, concat_axis=0, tiled=True),
        lax.all_to_all(send_gates, "eg", split_axis=0, concat_axis=0, tiled=True),
    )
    wgate = dequantize(gate_codes[0], block_scales[0, 0])
    wup = dequantize(up_codes[0], block_scales[0, 1])
    wdown = dequantize(down_codes[0], block_scales[0, 2])
    all_tokens, all_cotan, all_gates = (
        lax.all_gather(recv_tokens, "blk", axis=0, tiled=True),
        lax.all_gather(recv_cotan, "blk", axis=0, tiled=True),
        lax.all_gather(recv_gates, "blk", axis=0, tiled=True),
    )
    feats = all_tokens.reshape(-1, width)
    cotan = all_cotan.reshape(-1, width)
    gates = all_gates.reshape(-1).astype(jnp.float32)
    gate_pre = jnp.dot(feats, wgate, preferred_element_type=jnp.float32)
    up_pre = jnp.dot(feats, wup, preferred_element_type=jnp.float32)
    down_back = jnp.dot(cotan, wdown, preferred_element_type=jnp.float32)
    hidden, grad_gate, grad_up, gated_hidden = backward_math(gate_pre, up_pre, down_back, gates)
    contrib = project_back(grad_gate, grad_up, wgate, wup)
    scores = jnp.sum(hidden * down_back, axis=1)
    contrib, scores, grad_gate, grad_up, gated_hidden, feats, cotan = (
        contrib,
        scores,
        grad_gate,
        grad_up,
        gated_hidden,
        feats,
        cotan,
    )
    slots = contrib.shape[0] // capacity
    summed_rows, summed_scores = (
        lax.psum_scatter(
            contrib.reshape(slots, capacity, width).astype(jnp.bfloat16),
            "blk",
            scatter_dimension=0,
            tiled=True,
        ).astype(jnp.float32),
        lax.psum_scatter(
            scores.reshape(slots, capacity).astype(jnp.bfloat16),
            "blk",
            scatter_dimension=0,
            tiled=True,
        ).astype(jnp.float32),
    )
    back_rows = summed_rows.astype(jnp.bfloat16)
    back_gates = summed_scores.astype(jnp.bfloat16)
    gate_grad = row_sum(feats, grad_gate).astype(jnp.bfloat16)[None]
    up_grad = row_sum(feats, grad_up).astype(jnp.bfloat16)[None]
    down_grad = row_sum(cotan, gated_hidden).astype(jnp.bfloat16)[None]
    home_rows, home_gates = (
        lax.all_to_all(back_rows, "eg", split_axis=0, concat_axis=0, tiled=True),
        lax.all_to_all(back_gates, "eg", split_axis=0, concat_axis=0, tiled=True),
    )
    grad_tokens = jnp.einsum(
        "tec,ecd->td", placed_low, home_rows, preferred_element_type=jnp.float32
    ).astype(jnp.bfloat16)
    grad_gates = jnp.einsum(
        "tkec,ec->tk", picked, home_gates.astype(jnp.float32), precision=lax.Precision.HIGHEST
    ).astype(jnp.bfloat16)
    return (grad_tokens, grad_gates, gate_grad, up_grad, down_grad)


def solution(mesh):
    in_specs = (
        P(("eg", "blk"), None),
        P(("eg", "blk"), None),
        P(("eg", "blk"), None),
        P(("eg", "blk"), None),
        P("eg", None, "blk"),
        P("eg", None, "blk"),
        P("eg", None, "blk"),
        P("eg", None, "blk", None),
    )
    out_specs = (
        P(("eg", "blk"), None),
        P(("eg", "blk"), None),
        P("eg", None, "blk"),
        P("eg", None, "blk"),
        P("eg", None, "blk"),
    )
    return jax.shard_map(
        on_device, mesh=mesh, in_specs=in_specs, out_specs=out_specs, check_vma=False
    )
```

```python
import functools

import jax
import jax.numpy as jnp
from jax import lax
from jax.experimental import pallas as pl
from jax.experimental.pallas import tpu as pltpu
from jax.sharding import PartitionSpec as P

QBLOCK = 128
TOPK = 2


def backward_math(gate_pre, up_pre, down_back, gates):
    sigma = jax.nn.sigmoid(gate_pre)
    hidden = gate_pre * sigma * up_pre
    grad_hidden = gates * down_back
    grad_up = (grad_hidden * gate_pre * sigma).astype(jnp.bfloat16)
    grad_gate = (grad_hidden * up_pre * sigma * (1.0 + gate_pre * (1.0 - sigma))).astype(
        jnp.bfloat16
    )
    gated_hidden = (gates * hidden).astype(jnp.bfloat16)
    return (hidden, grad_gate, grad_up, gated_hidden)


def routing_tables(expert_ids, experts, capacity):
    route_hot = (
        expert_ids[:, :, None] == jnp.arange(experts, dtype=jnp.int32)[None, None, :]
    ).astype(jnp.int32)
    chosen = jnp.sum(route_hot, axis=1)
    rows = jnp.arange(expert_ids.shape[0], dtype=jnp.int32)
    before = (rows[None, :] < rows[:, None]).astype(jnp.int32)
    earlier = jnp.sum(before[:, :, None] * chosen[None, :, :], axis=1)
    slot_hot = (earlier[:, :, None] == jnp.arange(capacity, dtype=jnp.int32)[None, None, :]).astype(
        jnp.int32
    )
    placed = chosen[:, :, None] * slot_hot
    picked = route_hot[:, :, :, None] * slot_hot[:, None, :, :]
    return (placed.astype(jnp.float32), picked.astype(jnp.float32))


LANES = 128
NT = (((1,), (1,)), ((), ()))
TN = (((0,), (0,)), ((), ()))
f32, bf16 = jnp.float32, jnp.bfloat16


def expert_kernel(
    steps, x_ref, y_ref, gates_ref, scales_ref, gate_ref, up_ref, down_ref,
    back_ref, dgate_ref, dup_ref, gated_ref,
    wgate, wup, acc_gate, acc_up, acc_down,
):
    j = pl.program_id(0)
    chunk = x_ref.shape[1]
    blocks = chunk // QBLOCK
    hid = gate_ref.shape[2]

    @pl.when(j == 0)
    def _():
        acc_gate[...] = jnp.zeros_like(acc_gate)
        acc_up[...] = jnp.zeros_like(acc_up)
        acc_down[...] = jnp.zeros_like(acc_down)

    def scaled(ref, m):
        parts = []
        for b in range(blocks):
            row = m * blocks + b
            scale = jnp.broadcast_to(scales_ref[0, row : row + 1, :], (QBLOCK, hid)).astype(bf16)
            parts.append(ref[0, b * QBLOCK : (b + 1) * QBLOCK, :] * scale)
        return jnp.concatenate(parts, axis=0)

    place = pl.ds(pl.multiple_of(j * chunk, chunk), chunk)
    wg = scaled(gate_ref, 0)
    wgate[place, :] = wg
    acc_gate[...] += jnp.dot(x_ref[...], wg, preferred_element_type=f32)
    wu = scaled(up_ref, 1)
    wup[place, :] = wu
    acc_up[...] += jnp.dot(x_ref[...], wu, preferred_element_type=f32)
    acc_down[...] += jnp.dot(y_ref[...], scaled(down_ref, 2), preferred_element_type=f32)

    @pl.when(j == steps - 1)
    def _():
        gates = gates_ref[:, 0:1].astype(f32)
        hidden, dgate, dup, gated = backward_math(acc_gate[...], acc_up[...], acc_down[...], gates)
        dgate_ref[...] = dgate
        dup_ref[...] = dup
        gated_ref[...] = gated
        scores = jnp.sum(hidden * acc_down[...], axis=1, keepdims=True)
        width = steps * chunk
        back_ref[:, width : width + LANES] = jnp.broadcast_to(
            scores, (scores.shape[0], LANES)
        ).astype(bf16)

        @pl.loop(0, steps)
        def _(i):
            at = pl.ds(pl.multiple_of(i * chunk, chunk), chunk)
            total = lax.dot_general(dgate_ref[...], wgate[at, :], NT, preferred_element_type=f32)
            total += lax.dot_general(dup_ref[...], wup[at, :], NT, preferred_element_type=f32)
            back_ref[:, at] = total.astype(bf16)


def grads_kernel(x_ref, y_ref, dgate_ref, dup_ref, gated_ref, gate_ref, up_ref, down_ref):
    x = x_ref[...]
    gate_ref[0] = lax.dot_general(x, dgate_ref[...], TN, preferred_element_type=f32).astype(bf16)
    up_ref[0] = lax.dot_general(x, dup_ref[...], TN, preferred_element_type=f32).astype(bf16)
    down_ref[0] = lax.dot_general(
        y_ref[...], gated_ref[...], TN, preferred_element_type=f32
    ).astype(bf16)


def expert_part(rows, scales, gate_codes, up_codes, down_codes, chunk):
    count = rows.shape[0]
    _, width, hid = gate_codes.shape
    steps = width // chunk
    x_spec = pl.BlockSpec((count, chunk), lambda j: (0, j))
    y_spec = pl.BlockSpec((count, chunk), lambda j: (0, steps + j))
    code_spec = pl.BlockSpec((1, chunk, hid), lambda j: (0, j, 0))
    whole = pl.BlockSpec((count, hid), lambda j: (0, 0))
    small = jax.ShapeDtypeStruct((count, hid), bf16)
    return pl.pallas_call(
        functools.partial(expert_kernel, steps),
        grid=(steps,),
        in_specs=[
            x_spec,
            y_spec,
            pl.BlockSpec((count, LANES), lambda j: (0, 2 * width // LANES)),
            pl.BlockSpec((1, scales.shape[1], hid), lambda j: (j, 0, 0)),
            code_spec,
            code_spec,
            code_spec,
        ],
        out_specs=[
            pl.BlockSpec((count, width + LANES), lambda j: (0, 0)),
            whole,
            whole,
            whole,
        ],
        out_shape=[jax.ShapeDtypeStruct((count, width + LANES), bf16), small, small, small],
        scratch_shapes=[pltpu.VMEM((width, hid), bf16)] * 2 + [pltpu.VMEM((count, hid), f32)] * 3,
        compiler_params=pltpu.CompilerParams(vmem_limit_bytes=48 << 20),
        cost_estimate=pl.CostEstimate(
            flops=10 * count * width * hid,
            bytes_accessed=6 * width * hid + 6 * count * width,
            transcendentals=count * hid,
        ),
        name="expert",
    )(rows, rows, rows, scales, gate_codes, up_codes, down_codes)


def grads_part(rows, dgate, dup, gated, width, chunk):
    count, hid = dgate.shape
    steps = width // chunk
    whole = pl.BlockSpec((count, hid), lambda j: (0, 0))
    out = pl.BlockSpec((1, chunk, hid), lambda j: (0, j, 0))
    return pl.pallas_call(
        grads_kernel,
        grid=(steps,),
        in_specs=[
            pl.BlockSpec((count, chunk), lambda j: (0, j)),
            pl.BlockSpec((count, chunk), lambda j: (0, steps + j)),
            whole,
            whole,
            whole,
        ],
        out_specs=[out, out, out],
        out_shape=[jax.ShapeDtypeStruct((1, width, hid), bf16)] * 3,
        compiler_params=pltpu.CompilerParams(vmem_limit_bytes=56 << 20),
        cost_estimate=pl.CostEstimate(
            flops=6 * count * width * hid,
            bytes_accessed=6 * width * hid + 4 * count * width,
            transcendentals=0,
        ),
        name="grads",
    )(rows, rows, dgate, dup, gated)


def on_device(
    tokens, grad_out, expert_ids, gate_weights, gate_codes, up_codes, down_codes, block_scales
):
    experts = lax.axis_size("eg")
    width = tokens.shape[1]
    chunk = max(c for c in range(QBLOCK, 1024 + 1, QBLOCK) if width % c == 0)
    capacity = 2 * tokens.shape[0] * TOPK // experts
    slots = experts * capacity
    placed, picked = routing_tables(expert_ids, experts, capacity)
    flat = placed.astype(bf16).reshape(-1, slots)
    flat_picked = picked.reshape(-1, TOPK, slots)
    gates = jnp.sum(flat_picked * gate_weights.astype(f32)[:, :, None], axis=(0, 1))
    both = jnp.concatenate([tokens, grad_out], axis=1)
    sent = lax.dot_general(flat, both, TN, preferred_element_type=f32).astype(bf16)
    sent = jnp.concatenate(
        [sent, jnp.broadcast_to(gates.astype(bf16)[:, None], (slots, LANES))], axis=1
    )
    received = lax.all_to_all(
        sent.reshape(experts, capacity, -1), "eg", split_axis=0, concat_axis=0, tiled=True
    )
    rows = lax.all_gather(received.reshape(slots, -1), "blk", axis=0, tiled=True)

    hid = gate_codes.shape[2]
    scales = jnp.repeat(jnp.swapaxes(block_scales[0], 1, 2).astype(f32), QBLOCK, axis=2)
    scales = scales.reshape(3, width // chunk, chunk // QBLOCK, hid)
    scales = jnp.swapaxes(scales, 0, 1).reshape(width // chunk, -1, hid)
    back, dgate, dup, gated = expert_part(rows, scales, gate_codes, up_codes, down_codes, chunk)
    summed = lax.psum_scatter(back, "blk", scatter_dimension=0, tiled=True)
    gate_grad, up_grad, down_grad = grads_part(rows, dgate, dup, gated, width, chunk)
    summed, gate_grad, up_grad, down_grad = lax.optimization_barrier(
        (summed, gate_grad, up_grad, down_grad)
    )
    home = lax.all_to_all(
        summed.reshape(experts, capacity, -1), "eg", split_axis=0, concat_axis=0, tiled=True
    ).reshape(slots, -1)
    grad_tokens = jnp.dot(flat, home[:, :width], preferred_element_type=f32).astype(bf16)
    home_scores = home[:, width].astype(f32)
    grad_gates = jnp.sum(flat_picked * home_scores[None, None, :], axis=2).astype(bf16)
    return (grad_tokens, grad_gates, gate_grad, up_grad, down_grad)


def solution(mesh):
    in_specs = (
        P(("eg", "blk"), None),
        P(("eg", "blk"), None),
        P(("eg", "blk"), None),
        P(("eg", "blk"), None),
        P("eg", None, "blk"),
        P("eg", None, "blk"),
        P("eg", None, "blk"),
        P("eg", None, "blk", None),
    )
    out_specs = (
        P(("eg", "blk"), None),
        P(("eg", "blk"), None),
        P("eg", None, "blk"),
        P("eg", None, "blk"),
        P("eg", None, "blk"),
    )
    return jax.shard_map(
        on_device, mesh=mesh, in_specs=in_specs, out_specs=out_specs, check_vma=False
    )
```

```python
import functools

import jax
import jax.numpy as jnp
from jax import lax
from jax.experimental import pallas as pl
from jax.experimental.pallas import tpu as pltpu
from jax.sharding import PartitionSpec as P

QBLOCK = 128
TOPK = 2


def backward_math(gate_pre, up_pre, down_back, gates):
    sigma = jax.nn.sigmoid(gate_pre)
    hidden = gate_pre * sigma * up_pre
    grad_hidden = gates * down_back
    grad_up = (grad_hidden * gate_pre * sigma).astype(jnp.bfloat16)
    grad_gate = (grad_hidden * up_pre * sigma * (1.0 + gate_pre * (1.0 - sigma))).astype(
        jnp.bfloat16
    )
    gated_hidden = (gates * hidden).astype(jnp.bfloat16)
    return (hidden, grad_gate, grad_up, gated_hidden)


def routing_tables(expert_ids, experts, capacity):
    route_hot = (
        expert_ids[:, :, None] == jnp.arange(experts, dtype=jnp.int32)[None, None, :]
    ).astype(jnp.int32)
    chosen = jnp.sum(route_hot, axis=1)
    rows = jnp.arange(expert_ids.shape[0], dtype=jnp.int32)
    before = (rows[None, :] < rows[:, None]).astype(jnp.int32)
    earlier = jnp.sum(before[:, :, None] * chosen[None, :, :], axis=1)
    slot_hot = (earlier[:, :, None] == jnp.arange(capacity, dtype=jnp.int32)[None, None, :]).astype(
        jnp.int32
    )
    placed = chosen[:, :, None] * slot_hot
    picked = route_hot[:, :, :, None] * slot_hot[:, None, :, :]
    return (placed.astype(jnp.float32), picked.astype(jnp.float32))


LANES = 128
NT = (((1,), (1,)), ((), ()))
TN = (((0,), (0,)), ((), ()))
f32, bf16 = jnp.float32, jnp.bfloat16


def expert_kernel(
    steps, x_ref, y_ref, gates_ref, scales_ref, gate_ref, up_ref, down_ref,
    back_ref, dgate_ref, dup_ref, gated_ref,
    wgate, wup, acc_gate, acc_up, acc_down,
):
    j = pl.program_id(0)
    chunk = x_ref.shape[1]
    blocks = chunk // QBLOCK
    hid = gate_ref.shape[2]

    @pl.when(j == 0)
    def _():
        acc_gate[...] = jnp.zeros_like(acc_gate)
        acc_up[...] = jnp.zeros_like(acc_up)
        acc_down[...] = jnp.zeros_like(acc_down)

    def scaled(ref, m):
        parts = []
        for b in range(blocks):
            row = m * blocks + b
            scale = jnp.broadcast_to(scales_ref[0, row : row + 1, :], (QBLOCK, hid)).astype(bf16)
            parts.append(ref[0, b * QBLOCK : (b + 1) * QBLOCK, :] * scale)
        return jnp.concatenate(parts, axis=0)

    place = pl.ds(pl.multiple_of(j * chunk, chunk), chunk)
    wg = scaled(gate_ref, 0)
    wgate[place, :] = wg
    acc_gate[...] += jnp.dot(x_ref[...], wg, preferred_element_type=f32)
    wu = scaled(up_ref, 1)
    wup[place, :] = wu
    acc_up[...] += jnp.dot(x_ref[...], wu, preferred_element_type=f32)
    acc_down[...] += jnp.dot(y_ref[...], scaled(down_ref, 2), preferred_element_type=f32)

    @pl.when(j == steps - 1)
    def _():
        gates = gates_ref[:, 0:1].astype(f32)
        hidden, dgate, dup, gated = backward_math(acc_gate[...], acc_up[...], acc_down[...], gates)
        dgate_ref[...] = dgate
        dup_ref[...] = dup
        gated_ref[...] = gated
        scores = jnp.sum(hidden * acc_down[...], axis=1, keepdims=True)
        width = steps * chunk
        back_ref[:, width : width + LANES] = jnp.broadcast_to(
            scores, (scores.shape[0], LANES)
        ).astype(bf16)

        @pl.loop(0, steps)
        def _(i):
            at = pl.ds(pl.multiple_of(i * chunk, chunk), chunk)
            total = lax.dot_general(dgate_ref[...], wgate[at, :], NT, preferred_element_type=f32)
            total += lax.dot_general(dup_ref[...], wup[at, :], NT, preferred_element_type=f32)
            back_ref[:, at] = total.astype(bf16)


def grads_kernel(x_ref, y_ref, dgate_ref, dup_ref, gated_ref, gate_ref, up_ref, down_ref):
    x = x_ref[...]
    gate_ref[0] = lax.dot_general(x, dgate_ref[...], TN, preferred_element_type=f32).astype(bf16)
    up_ref[0] = lax.dot_general(x, dup_ref[...], TN, preferred_element_type=f32).astype(bf16)
    down_ref[0] = lax.dot_general(
        y_ref[...], gated_ref[...], TN, preferred_element_type=f32
    ).astype(bf16)


def expert_part(rows, cotan, scales, gate_codes, up_codes, down_codes, chunk):
    count = rows.shape[0]
    _, width, hid = gate_codes.shape
    steps = width // chunk
    x_spec = pl.BlockSpec((count, chunk), lambda j: (0, j))
    y_spec = pl.BlockSpec((count, chunk), lambda j: (0, j))
    code_spec = pl.BlockSpec((1, chunk, hid), lambda j: (0, j, 0))
    whole = pl.BlockSpec((count, hid), lambda j: (0, 0))
    small = jax.ShapeDtypeStruct((count, hid), bf16)
    return pl.pallas_call(
        functools.partial(expert_kernel, steps),
        grid=(steps,),
        in_specs=[
            x_spec,
            y_spec,
            pl.BlockSpec((count, LANES), lambda j: (0, width // LANES)),
            pl.BlockSpec((1, scales.shape[1], hid), lambda j: (j, 0, 0)),
            code_spec,
            code_spec,
            code_spec,
        ],
        out_specs=[
            pl.BlockSpec((count, width + LANES), lambda j: (0, 0)),
            whole,
            whole,
            whole,
        ],
        out_shape=[jax.ShapeDtypeStruct((count, width + LANES), bf16), small, small, small],
        scratch_shapes=[pltpu.VMEM((width, hid), bf16)] * 2 + [pltpu.VMEM((count, hid), f32)] * 3,
        compiler_params=pltpu.CompilerParams(vmem_limit_bytes=48 << 20),
        cost_estimate=pl.CostEstimate(
            flops=10 * count * width * hid,
            bytes_accessed=6 * width * hid + 6 * count * width,
            transcendentals=count * hid,
        ),
        name="expert",
    )(rows, cotan, cotan, scales, gate_codes, up_codes, down_codes)


def grads_part(rows, cotan, dgate, dup, gated, width, chunk):
    count, hid = dgate.shape
    steps = width // chunk
    whole = pl.BlockSpec((count, hid), lambda j: (0, 0))
    out = pl.BlockSpec((1, chunk, hid), lambda j: (0, j, 0))
    return pl.pallas_call(
        grads_kernel,
        grid=(steps,),
        in_specs=[
            pl.BlockSpec((count, chunk), lambda j: (0, j)),
            pl.BlockSpec((count, chunk), lambda j: (0, j)),
            whole,
            whole,
            whole,
        ],
        out_specs=[out, out, out],
        out_shape=[jax.ShapeDtypeStruct((1, width, hid), bf16)] * 3,
        compiler_params=pltpu.CompilerParams(vmem_limit_bytes=56 << 20),
        cost_estimate=pl.CostEstimate(
            flops=6 * count * width * hid,
            bytes_accessed=6 * width * hid + 4 * count * width,
            transcendentals=0,
        ),
        name="grads",
    )(rows, cotan, dgate, dup, gated)


def on_device(
    tokens, grad_out, expert_ids, gate_weights, gate_codes, up_codes, down_codes, block_scales
):
    experts = lax.axis_size("eg")
    width = tokens.shape[1]
    chunk = max(c for c in range(QBLOCK, 1024 + 1, QBLOCK) if width % c == 0)
    capacity = 2 * tokens.shape[0] * TOPK // experts
    slots = experts * capacity
    placed, picked = routing_tables(expert_ids, experts, capacity)
    flat = placed.astype(bf16).reshape(-1, slots)
    flat_picked = picked.reshape(-1, TOPK, slots)
    gates = jnp.sum(flat_picked * gate_weights.astype(f32)[:, :, None], axis=(0, 1))

    def exchange(sent):
        received = lax.all_to_all(
            sent.reshape(experts, capacity, -1), "eg", split_axis=0, concat_axis=0, tiled=True
        )
        return received.reshape(slots, -1)

    sent = lax.dot_general(flat, tokens, TN, preferred_element_type=f32).astype(bf16)
    received = exchange(sent)
    sent = lax.dot_general(flat, grad_out, TN, preferred_element_type=f32).astype(bf16)
    sent = jnp.concatenate(
        [sent, jnp.broadcast_to(gates.astype(bf16)[:, None], (slots, LANES))], axis=1
    )
    received, sent = lax.optimization_barrier((received, sent))
    rows = lax.all_gather(received, "blk", axis=0, tiled=True)
    cotan = lax.all_gather(exchange(sent), "blk", axis=0, tiled=True)

    hid = gate_codes.shape[2]
    scales = jnp.repeat(jnp.swapaxes(block_scales[0], 1, 2).astype(f32), QBLOCK, axis=2)
    scales = scales.reshape(3, width // chunk, chunk // QBLOCK, hid)
    scales = jnp.swapaxes(scales, 0, 1).reshape(width // chunk, -1, hid)
    back, dgate, dup, gated = expert_part(rows, cotan, scales, gate_codes, up_codes, down_codes, chunk)
    summed = lax.psum_scatter(back, "blk", scatter_dimension=0, tiled=True)
    gate_grad, up_grad, down_grad = grads_part(rows, cotan, dgate, dup, gated, width, chunk)
    summed, gate_grad, up_grad, down_grad = lax.optimization_barrier(
        (summed, gate_grad, up_grad, down_grad)
    )
    home = lax.all_to_all(
        summed.reshape(experts, capacity, -1), "eg", split_axis=0, concat_axis=0, tiled=True
    ).reshape(slots, -1)
    grad_tokens = jnp.dot(flat, home[:, :width], preferred_element_type=f32).astype(bf16)
    home_scores = home[:, width].astype(f32)
    grad_gates = jnp.sum(flat_picked * home_scores[None, None, :], axis=2).astype(bf16)
    return (grad_tokens, grad_gates, gate_grad, up_grad, down_grad)


def solution(mesh):
    in_specs = (
        P(("eg", "blk"), None),
        P(("eg", "blk"), None),
        P(("eg", "blk"), None),
        P(("eg", "blk"), None),
        P("eg", None, "blk"),
        P("eg", None, "blk"),
        P("eg", None, "blk"),
        P("eg", None, "blk", None),
    )
    out_specs = (
        P(("eg", "blk"), None),
        P(("eg", "blk"), None),
        P("eg", None, "blk"),
        P("eg", None, "blk"),
        P("eg", None, "blk"),
    )
    return jax.shard_map(
        on_device, mesh=mesh, in_specs=in_specs, out_specs=out_specs, check_vma=False
    )
```

```python
import functools

import jax
import jax.numpy as jnp
from jax import lax
from jax.experimental import pallas as pl
from jax.experimental.pallas import tpu as pltpu
from jax.sharding import PartitionSpec as P

QBLOCK = 128
TOPK = 2


def backward_math(gate_pre, up_pre, down_back, gates):
    sigma = jax.nn.sigmoid(gate_pre)
    hidden = gate_pre * sigma * up_pre
    grad_hidden = gates * down_back
    grad_up = (grad_hidden * gate_pre * sigma).astype(jnp.bfloat16)
    grad_gate = (grad_hidden * up_pre * sigma * (1.0 + gate_pre * (1.0 - sigma))).astype(
        jnp.bfloat16
    )
    gated_hidden = (gates * hidden).astype(jnp.bfloat16)
    return (hidden, grad_gate, grad_up, gated_hidden)


def routing_tables(expert_ids, experts, capacity):
    route_hot = (
        expert_ids[:, :, None] == jnp.arange(experts, dtype=jnp.int32)[None, None, :]
    ).astype(jnp.int32)
    chosen = jnp.sum(route_hot, axis=1)
    rows = jnp.arange(expert_ids.shape[0], dtype=jnp.int32)
    before = (rows[None, :] < rows[:, None]).astype(jnp.int32)
    earlier = jnp.sum(before[:, :, None] * chosen[None, :, :], axis=1)
    slot_hot = (earlier[:, :, None] == jnp.arange(capacity, dtype=jnp.int32)[None, None, :]).astype(
        jnp.int32
    )
    placed = chosen[:, :, None] * slot_hot
    picked = route_hot[:, :, :, None] * slot_hot[:, None, :, :]
    return (placed.astype(jnp.float32), picked.astype(jnp.float32))


LANES = 128
NT = (((1,), (1,)), ((), ()))
TN = (((0,), (0,)), ((), ()))
f32, bf16 = jnp.float32, jnp.bfloat16


def expert_kernel(
    steps, x_ref, y_ref, gates_ref, scales_ref, gate_ref, up_ref, down_ref,
    back_ref, dgate_ref, dup_ref, gated_ref,
    wgate, wup, acc_gate, acc_up, acc_down,
):
    j = pl.program_id(0)
    chunk = x_ref.shape[1]
    blocks = chunk // QBLOCK
    hid = gate_ref.shape[2]

    @pl.when(j == 0)
    def _():
        acc_gate[...] = jnp.zeros_like(acc_gate)
        acc_up[...] = jnp.zeros_like(acc_up)
        acc_down[...] = jnp.zeros_like(acc_down)

    def scaled(ref, m):
        parts = []
        for b in range(blocks):
            row = m * blocks + b
            scale = jnp.broadcast_to(scales_ref[0, row : row + 1, :], (QBLOCK, hid)).astype(bf16)
            parts.append(ref[0, b * QBLOCK : (b + 1) * QBLOCK, :] * scale)
        return jnp.concatenate(parts, axis=0)

    place = pl.ds(pl.multiple_of(j * chunk, chunk), chunk)
    wg = scaled(gate_ref, 0)
    wgate[place, :] = wg
    acc_gate[...] += jnp.dot(x_ref[...], wg, preferred_element_type=f32)
    wu = scaled(up_ref, 1)
    wup[place, :] = wu
    acc_up[...] += jnp.dot(x_ref[...], wu, preferred_element_type=f32)
    acc_down[...] += jnp.dot(y_ref[...], scaled(down_ref, 2), preferred_element_type=f32)

    @pl.when(j == steps - 1)
    def _():
        gates = gates_ref[:, 0:1].astype(f32)
        hidden, dgate, dup, gated = backward_math(acc_gate[...], acc_up[...], acc_down[...], gates)
        dgate_ref[...] = dgate
        dup_ref[...] = dup
        gated_ref[...] = gated
        scores = jnp.sum(hidden * acc_down[...], axis=1, keepdims=True)
        width = steps * chunk
        back_ref[:, width : width + LANES] = jnp.broadcast_to(
            scores, (scores.shape[0], LANES)
        ).astype(bf16)

        @pl.loop(0, steps)
        def _(i):
            at = pl.ds(pl.multiple_of(i * chunk, chunk), chunk)
            total = lax.dot_general(dgate_ref[...], wgate[at, :], NT, preferred_element_type=f32)
            total += lax.dot_general(dup_ref[...], wup[at, :], NT, preferred_element_type=f32)
            back_ref[:, at] = total.astype(bf16)


def grads_kernel(x_ref, y_ref, dgate_ref, dup_ref, gated_ref, gate_ref, up_ref, down_ref):
    x = x_ref[...]
    gate_ref[0] = lax.dot_general(x, dgate_ref[...], TN, preferred_element_type=f32).astype(bf16)
    up_ref[0] = lax.dot_general(x, dup_ref[...], TN, preferred_element_type=f32).astype(bf16)
    down_ref[0] = lax.dot_general(
        y_ref[...], gated_ref[...], TN, preferred_element_type=f32
    ).astype(bf16)


def expert_part(rows, cotan, scales, gate_codes, up_codes, down_codes, chunk):
    count = rows.shape[0]
    _, width, hid = gate_codes.shape
    steps = width // chunk
    x_spec = pl.BlockSpec((count, chunk), lambda j: (0, j))
    y_spec = pl.BlockSpec((count, chunk), lambda j: (0, j))
    code_spec = pl.BlockSpec((1, chunk, hid), lambda j: (0, j, 0))
    whole = pl.BlockSpec((count, hid), lambda j: (0, 0))
    small = jax.ShapeDtypeStruct((count, hid), bf16)
    return pl.pallas_call(
        functools.partial(expert_kernel, steps),
        grid=(steps,),
        in_specs=[
            x_spec,
            y_spec,
            pl.BlockSpec((count, LANES), lambda j: (0, width // LANES)),
            pl.BlockSpec((1, scales.shape[1], hid), lambda j: (j, 0, 0)),
            code_spec,
            code_spec,
            code_spec,
        ],
        out_specs=[
            pl.BlockSpec((count, width + LANES), lambda j: (0, 0)),
            whole,
            whole,
            whole,
        ],
        out_shape=[jax.ShapeDtypeStruct((count, width + LANES), bf16), small, small, small],
        scratch_shapes=[pltpu.VMEM((width, hid), bf16)] * 2 + [pltpu.VMEM((count, hid), f32)] * 3,
        compiler_params=pltpu.CompilerParams(vmem_limit_bytes=48 << 20),
        cost_estimate=pl.CostEstimate(
            flops=10 * count * width * hid,
            bytes_accessed=6 * width * hid + 6 * count * width,
            transcendentals=count * hid,
        ),
        name="expert",
    )(rows, cotan, cotan, scales, gate_codes, up_codes, down_codes)


def grads_part(rows, cotan, dgate, dup, gated, width, chunk):
    count, hid = dgate.shape
    steps = width // chunk
    whole = pl.BlockSpec((count, hid), lambda j: (0, 0))
    out = pl.BlockSpec((1, chunk, hid), lambda j: (0, j, 0))
    return pl.pallas_call(
        grads_kernel,
        grid=(steps,),
        in_specs=[
            pl.BlockSpec((count, chunk), lambda j: (0, j)),
            pl.BlockSpec((count, chunk), lambda j: (0, j)),
            whole,
            whole,
            whole,
        ],
        out_specs=[out, out, out],
        out_shape=[jax.ShapeDtypeStruct((1, width, hid), bf16)] * 3,
        compiler_params=pltpu.CompilerParams(vmem_limit_bytes=56 << 20),
        cost_estimate=pl.CostEstimate(
            flops=6 * count * width * hid,
            bytes_accessed=6 * width * hid + 4 * count * width,
            transcendentals=0,
        ),
        name="grads",
    )(rows, cotan, dgate, dup, gated)


def shifted(value, step):
    count = lax.axis_size("blk")
    return lax.ppermute(value, "blk", [(i, (i + 2 * step) % count) for i in range(count)])


def other_core(value):
    count = lax.axis_size("blk")
    return lax.ppermute(value, "blk", [(i, i ^ 1) for i in range(count)])


def gather_rows(own):
    chips = lax.axis_size("blk") // 2
    mine = jnp.concatenate([own] + [shifted(own, step) for step in range(1, chips)], axis=0)
    return jnp.concatenate([mine, other_core(mine)], axis=0)


def return_rows(back):
    chips = lax.axis_size("blk") // 2
    half = back.shape[0] // 2
    size = half // chips
    sums = back[:half].astype(f32) + other_core(back[half:]).astype(f32)
    sums = sums.astype(bf16)
    total = sums[:size].astype(f32)
    for step in range(1, chips):
        total += shifted(sums[step * size : (step + 1) * size], -step).astype(f32)
    return total.astype(bf16)


def on_device(
    tokens, grad_out, expert_ids, gate_weights, gate_codes, up_codes, down_codes, block_scales
):
    experts = lax.axis_size("eg")
    width = tokens.shape[1]
    chunk = max(c for c in range(QBLOCK, 1024 + 1, QBLOCK) if width % c == 0)
    capacity = 2 * tokens.shape[0] * TOPK // experts
    slots = experts * capacity
    placed, picked = routing_tables(expert_ids, experts, capacity)
    flat = placed.astype(bf16).reshape(-1, slots)
    flat_picked = picked.reshape(-1, TOPK, slots)
    gates = jnp.sum(flat_picked * gate_weights.astype(f32)[:, :, None], axis=(0, 1))

    def exchange(sent):
        received = lax.all_to_all(
            sent.reshape(experts, capacity, -1), "eg", split_axis=0, concat_axis=0, tiled=True
        )
        return received.reshape(slots, -1)

    sent = lax.dot_general(flat, tokens, TN, preferred_element_type=f32).astype(bf16)
    received = exchange(sent)
    sent = lax.dot_general(flat, grad_out, TN, preferred_element_type=f32).astype(bf16)
    sent = jnp.concatenate(
        [sent, jnp.broadcast_to(gates.astype(bf16)[:, None], (slots, LANES))], axis=1
    )
    received, sent = lax.optimization_barrier((received, sent))
    rows = gather_rows(received)
    cotan = gather_rows(exchange(sent))

    hid = gate_codes.shape[2]
    scales = jnp.repeat(jnp.swapaxes(block_scales[0], 1, 2).astype(f32), QBLOCK, axis=2)
    scales = scales.reshape(3, width // chunk, chunk // QBLOCK, hid)
    scales = jnp.swapaxes(scales, 0, 1).reshape(width // chunk, -1, hid)
    back, dgate, dup, gated = expert_part(rows, cotan, scales, gate_codes, up_codes, down_codes, chunk)
    summed = return_rows(back)
    gate_grad, up_grad, down_grad = grads_part(rows, cotan, dgate, dup, gated, width, chunk)
    summed, gate_grad, up_grad, down_grad = lax.optimization_barrier(
        (summed, gate_grad, up_grad, down_grad)
    )
    home = lax.all_to_all(
        summed.reshape(experts, capacity, -1), "eg", split_axis=0, concat_axis=0, tiled=True
    ).reshape(slots, -1)
    grad_tokens = jnp.dot(flat, home[:, :width], preferred_element_type=f32).astype(bf16)
    home_scores = home[:, width].astype(f32)
    grad_gates = jnp.sum(flat_picked * home_scores[None, None, :], axis=2).astype(bf16)
    return (grad_tokens, grad_gates, gate_grad, up_grad, down_grad)


def solution(mesh):
    in_specs = (
        P(("eg", "blk"), None),
        P(("eg", "blk"), None),
        P(("eg", "blk"), None),
        P(("eg", "blk"), None),
        P("eg", None, "blk"),
        P("eg", None, "blk"),
        P("eg", None, "blk"),
        P("eg", None, "blk", None),
    )
    out_specs = (
        P(("eg", "blk"), None),
        P(("eg", "blk"), None),
        P("eg", None, "blk"),
        P("eg", None, "blk"),
        P("eg", None, "blk"),
    )
    return jax.shard_map(
        on_device, mesh=mesh, in_specs=in_specs, out_specs=out_specs, check_vma=False
    )
```
